32 devices in a mesh: groups: 1, row: 16 (over z, y, core), chan: 2 (over x), sub: 1.
Axes of the slice: x: 2, y: 2, z: 4, core: 2. Of those that a mesh axis runs over, the one named last changes fastest.
Arguments:
- pair_act: bfloat16 [256, 256, 128], P(('groups', 'row'), 'sub'), may hold values from -6 to 6
- residue_valid: int32 [256], P('groups'), may hold values 0 or 1
- in_gain: float32 [128], replicated, may hold values from 0.1 to 1.9
- w_left: bfloat16 [128, 128], P(None, 'chan'), may hold values from -0.5 to 0.5
- w_left_gate: bfloat16 [128, 128], P(None, 'chan'), may hold values from -0.5 to 0.5
- w_right: bfloat16 [128, 128], P(None, 'chan'), may hold values from -0.5 to 0.5
- w_right_gate: bfloat16 [128, 128], P(None, 'chan'), may hold values from -0.5 to 0.5
- out_gain: float32 [128], replicated, may hold values from 0.1 to 1.9
- w_out: bfloat16 [128, 128], replicated, may hold values from -0.5 to 0.5
- w_out_gate: bfloat16 [128, 128], replicated, may hold values from -0.5 to 0.5
Outputs:
- update: bfloat16 [256, 256, 128], P(('groups', 'row'), 'sub')
The draws below stay inside these ranges and needn't reach their ends.
All inputs are finite; a program needn't handle non-finite values.
Results may differ from the reference program's by a relative error of at most 0.017.
Values may be sent and summed in bfloat16 or wider, within the bound.
A program may use at most 64 MiB of HBM per device.

```python
import jax
import jax.numpy as jnp
from jax import lax

C = 128
H = 128
N = 256


def plant(values, stream_key, low, largest):
    dims = values.shape
    place = [jax.random.randint(jax.random.fold_in(stream_key, axis), (), 0, dims[axis]) for axis in range(len(dims))]
    values = values.at[tuple(place)].set(low)
    longest = dims.index(max(dims))
    place[longest] = (place[longest] + 1) % dims[longest]
    return values.at[tuple(place)].set(largest)


def steps_of(stream_key, dims, shards, low, high):
    level = 1.0
    for position, shards_of in shards:
        draws = jax.random.uniform(jax.random.fold_in(jax.random.fold_in(stream_key, 6), position), (shards_of,), jnp.float32, low / len(shards), high / len(shards))
        level = level * jnp.repeat(jnp.exp(draws), dims[position] // shards_of).reshape((-1,) + (1,) * (len(dims) - 1 - position))
    return level


def gaussian(stream_key, shape, deviation, limit, split=(), kind=jnp.bfloat16):
    values = deviation * jax.random.normal(stream_key, shape, jnp.float32)
    if split:
        values = values * steps_of(stream_key, shape, split, -0.22, 0.18)
    return jnp.clip(values, -limit, limit).astype(kind)


def setup_inputs(seed: int = 0, part: int = 0) -> dict:
    key_list = jax.random.split(jax.random.key(seed), 11)
    own_keys = jax.random.split(jax.random.fold_in(key_list[10], part), 11)
    pair_act = gaussian(own_keys[0], (N, N, C), 1.0, 6.0, ((0, 16),))
    residue_valid = plant((jax.random.randint(own_keys[1], (N,), 0, 8) < 7).astype(jnp.int32), jax.random.fold_in(own_keys[1], 1), 0, 1)
    in_gain = jnp.clip(1.0 + 0.18 * jax.random.normal(key_list[2], (C,), jnp.float32), 0.1, 1.9)
    w_left = gaussian(key_list[3], (C, H), C ** -0.5, 0.5, ((1, 2),))
    w_left_gate = gaussian(key_list[4], (C, H), C ** -0.5, 0.5, ((1, 2),))
    w_right = gaussian(key_list[5], (C, H), C ** -0.5, 0.5, ((1, 2),))
    w_right_gate = gaussian(key_list[6], (C, H), C ** -0.5, 0.5, ((1, 2),))
    out_gain = jnp.clip(1.0 + 0.18 * jax.random.normal(key_list[7], (H,), jnp.float32), 0.1, 1.9)
    w_out = gaussian(key_list[8], (H, C), H ** -0.5, 0.5)
    w_out_gate = gaussian(key_list[9], (C, C), C ** -0.5, 0.5)
    return {"pair_act": pair_act, "residue_valid": residue_valid, "in_gain": in_gain, "w_left": w_left, "w_left_gate": w_left_gate, "w_right": w_right, "w_right_gate": w_right_gate, "out_gain": out_gain, "w_out": w_out, "w_out_gate": w_out_gate}


def norm_last(values, gain):
    mean = lax.optimization_barrier(jnp.mean(values, axis=-1, keepdims=True))
    centered = values - mean
    variance = lax.optimization_barrier(jnp.mean(centered * centered, axis=-1, keepdims=True))
    return centered * lax.rsqrt(variance + 1e-05) * gain

def reference(pair_act, residue_valid, in_gain, w_left, w_left_gate, w_right, w_right_gate, out_gain, w_out, w_out_gate):
    normed = norm_last(pair_act.astype(jnp.float32), in_gain).astype(jnp.bfloat16)
    flat = normed.reshape(N * N, C)
    valid = residue_valid.astype(jnp.float32)
    weight = (valid[:, None] * valid[None, :])[:, :, None]

    def project(w_lin, w_gate):
        linear = jnp.dot(flat, w_lin, preferred_element_type=jnp.float32).reshape(N, N, H)
        gating = jnp.dot(flat, w_gate, preferred_element_type=jnp.float32).reshape(N, N, H)
        return (jax.nn.sigmoid(gating) * linear * weight).astype(jnp.bfloat16)
    left = jnp.transpose(project(w_left, w_left_gate), (2, 0, 1)).astype(jnp.float32)
    right = jnp.transpose(project(w_right, w_right_gate), (2, 0, 1)).astype(jnp.float32)
    tri = jnp.einsum('hik,hjk->hij', left, right, precision=lax.Precision.HIGHEST)
    tri_round = lax.optimization_barrier(tri.astype(jnp.bfloat16))
    moved = jnp.transpose(tri_round.astype(jnp.float32), (1, 2, 0))
    tri_norm = norm_last(moved, out_gain).astype(jnp.bfloat16)
    projected = jnp.dot(tri_norm.reshape(N * N, H), w_out, preferred_element_type=jnp.float32)
    gating = jnp.dot(flat, w_out_gate, preferred_element_type=jnp.float32)
    return (jax.nn.sigmoid(gating) * projected).reshape(N, N, C).astype(jnp.bfloat16)
```

```python
import functools

import jax
import jax.numpy as jnp
from jax import lax
from jax.experimental import pallas as pl
from jax.experimental.pallas import tpu as pltpu
from jax.sharding import PartitionSpec as P

MESH = pl.DeviceIdType.MESH


def norm_axis(values, gain, axis):
    mean = jnp.mean(values, axis=axis, keepdims=True)
    centered = values - mean
    variance = jnp.mean(centered * centered, axis=axis, keepdims=True)
    return centered * lax.rsqrt(variance + 1e-05) * gain


def ring_orders(chunks, half):
    orders = []
    for way in range(2):
        order = []
        for first in range(0, chunks, 2):
            pair = [q for q in (first, first + 1) if q < chunks]
            block = [(q, d) for d in range(1, half + 1) for q in pair]
            block = [(q, d) for q, d in block if d < half or q % 2 == way]
            if order:
                tail = order.pop()
                order += [block[0], tail] + block[1:]
            else:
                order = block
        orders.append(order)
    return orders


def triangle_kernel(
    chips, chunks, left_ref, right_ref, tri_ref, held, lefts, part, sib_sem, ring_send, ring_recv, out_send, out_recv, local_sem
):
    rows = right_ref.shape[1]
    h_count = right_ref.shape[0]
    hc = h_count // chunks
    half = chips // 2
    index = lax.axis_index("row")
    x = lax.axis_index("chan")
    core = lax.rem(index, 2)
    chip = lax.div(index, 2)
    y = lax.rem(chip, 2)
    z = lax.div(chip, 2)
    place = jnp.where(y == 0, z, chips - 1 - z)

    def chip_at(ring_place):
        spot = lax.rem(ring_place + 2 * chips, chips)
        return jnp.where(spot < half, 2 * spot, 2 * (chips - 1 - spot) + 1)

    sibling = {"row": chip * 2 + (1 - core), "chan": x}
    nexts = [
        {"row": chip_at(place + 1) * 2 + core, "chan": x},
        {"row": chip_at(place - 1) * 2 + core, "chan": x},
    ]
    across = {"row": index, "chan": 1 - x}
    diagonal = {"row": chip * 2 + (1 - core), "chan": 1 - x}

    barrier = pltpu.get_barrier_semaphore()
    for partner in (sibling, nexts[0], nexts[1], across, diagonal):
        pl.semaphore_signal(barrier, inc=1, device_id=partner, device_id_type=MESH)
    pl.semaphore_wait(barrier, 5)

    def at_rows(block):
        return pl.ds(pl.multiple_of(block * rows, rows), rows)

    def ring_copy(way, q, d):
        step = 1 - 2 * way
        source = at_rows(chip_at(place - step * (d - 1)))
        heads = pl.ds(q * hc, hc)
        spot = held.at[heads, source]
        return pltpu.make_async_remote_copy(
            src_ref=right_ref.at[heads] if d == 1 else spot,
            dst_ref=spot,
            send_sem=ring_send.at[way, q, d - 1],
            recv_sem=ring_recv.at[way, q, d - 1],
            device_id=nexts[way],
            device_id_type=MESH,
        )

    left_copy = pltpu.make_async_remote_copy(
        src_ref=left_ref,
        dst_ref=lefts.at[:, at_rows(core)],
        send_sem=sib_sem.at[0],
        recv_sem=sib_sem.at[1],
        device_id=sibling,
        device_id_type=MESH,
    )

    def out_copies(q):
        heads = pl.ds(q * hc, hc)
        target = tri_ref.at[
            pl.ds(x * h_count + q * hc, hc), :, pl.ds(pl.multiple_of(core * rows * chips, 128), rows * chips)
        ]
        copies = []
        for n, (device, owner) in enumerate(((across, core), (diagonal, 1 - core), (sibling, 1 - core))):
            copies.append(
                pltpu.make_async_remote_copy(
                    src_ref=part.at[heads, at_rows(owner)],
                    dst_ref=target,
                    send_sem=out_send.at[n, q],
                    recv_sem=out_recv.at[n, q],
                    device_id=device,
                    device_id_type=MESH,
                )
            )
        own = pltpu.make_async_copy(part.at[heads, at_rows(core)], target, local_sem.at[q])
        return copies, own

    def compute(q):
        for way in range(2):
            top = half if q % 2 == way else half - 1
            for d in range(1, top + 1):
                if (way, q, d) not in waited:
                    ring_copy(way, q, d).wait_recv()
                    waited.add((way, q, d))
        heads = pl.ds(q * hc, hc)
        product = lax.dot_general(
            lefts[heads], held[heads], (((2,), (2,)), ((0,), (0,))), preferred_element_type=jnp.float32
        )
        part[heads] = product.astype(jnp.bfloat16)
        copies, own = out_copies(q)
        for copy in copies:
            copy.start()
        own.start()

    orders = ring_orders(chunks, half)
    waited = set()
    done = 0
    for n in range(len(orders[0])):
        for way in range(2):
            q, d = orders[way][n]
            if d > 1 and (way, q, d - 1) not in waited:
                ring_copy(way, q, d - 1).wait_recv()
                waited.add((way, q, d - 1))
            ring_copy(way, q, d).start()
        if n == 1:
            left_copy.start()
            held[:, at_rows(chip)] = right_ref[...]
            lefts[:, at_rows(core)] = left_ref[...]
        last = max(orders[w].index((done, half if done % 2 == w else half - 1)) for w in range(2))
        if n >= last + 2 and n < len(orders[0]) - 1:
            if done == 0:
                left_copy.wait_recv()
            compute(done)
            done += 1
    if done == 0:
        left_copy.wait_recv()
    while done < chunks:
        compute(done)
        done += 1
    for way in range(2):
        for q, d in orders[way]:
            ring_copy(way, q, d).wait_send()
    left_copy.wait_send()
    for q in range(chunks):
        copies, own = out_copies(q)
        for copy in copies:
            copy.wait()
        own.wait()


def triangle(left, right, row_devices, chunks):
    h_count, rows, depth = right.shape
    chips = row_devices // 2
    half = chips // 2
    dma = pltpu.SemaphoreType.DMA
    vmem = pl.BlockSpec(memory_space=pltpu.VMEM)
    return pl.pallas_call(
        functools.partial(triangle_kernel, chips, chunks),
        out_shape=jax.ShapeDtypeStruct((2 * h_count, rows, 2 * chips * rows), jnp.bfloat16),
        in_specs=[vmem, vmem],
        out_specs=vmem,
        scratch_shapes=[
            pltpu.VMEM((h_count, chips * rows, depth), jnp.bfloat16),
            pltpu.VMEM((h_count, 2 * rows, depth), jnp.bfloat16),
            pltpu.VMEM((h_count, 2 * rows, chips * rows), jnp.bfloat16),
            dma((2,)),
            dma((2, chunks, half)),
            dma((2, chunks, half)),
            dma((3, chunks)),
            dma((3, chunks)),
            dma((chunks,)),
        ],
        compiler_params=pltpu.CompilerParams(
            collective_id=0, has_side_effects=True, vmem_limit_bytes=40 * 1024 * 1024
        ),
        cost_estimate=pl.CostEstimate(
            flops=4 * h_count * rows * rows * chips * depth, bytes_accessed=8 * 1024 * 1024, transcendentals=0
        ),
    )(left, right)


def body(row_devices, chan_devices, sub_devices, *operands):
    pair_act, residue_valid, in_gain, w_left, w_left_gate, w_right, w_right_gate, out_gain, w_out, w_out_gate = operands
    row_count = pair_act.shape[0]
    col_count = pair_act.shape[1]
    row_first = lax.axis_index("row") * row_count
    col_first = lax.axis_index("sub") * col_count
    normed = norm_axis(pair_act.astype(jnp.float32), in_gain, 2).astype(jnp.bfloat16)
    valid = residue_valid.astype(jnp.float32)
    row_valid = lax.dynamic_slice_in_dim(valid, row_first, row_count)
    col_valid = lax.dynamic_slice_in_dim(valid, col_first, col_count)
    weight = (row_valid[:, None] * col_valid[None, :])[None, :, :]

    def project(w_lin, w_gate):
        linear = jnp.einsum("ikc,ch->hik", normed, w_lin, preferred_element_type=jnp.float32)
        gating = jnp.einsum("ikc,ch->hik", normed, w_gate, preferred_element_type=jnp.float32)
        return (jax.nn.sigmoid(gating) * linear * weight).astype(jnp.bfloat16)

    left = project(w_left, w_left_gate)
    right = project(w_right, w_right_gate)
    chips = row_devices // 2
    ringed = sub_devices == 1 and chan_devices == 2 and row_devices % 4 == 0 and (chips * row_count) % 128 == 0
    if ringed:
        tri_full = triangle(left, right, row_devices, 4)
    else:
        right_all = lax.all_gather(right, "row", axis=1, tiled=True)
        partial_tri = lax.dot_general(
            left, right_all, (((2,), (2,)), ((0,), (0,))), preferred_element_type=jnp.float32
        )
        tri_half = lax.psum_scatter(partial_tri.astype(jnp.bfloat16), "sub", scatter_dimension=2, tiled=True)
        tri_full = lax.all_gather(tri_half, "chan", axis=0, tiled=True)
    tri_norm = norm_axis(tri_full.astype(jnp.float32), out_gain[:, None, None], 0).astype(jnp.bfloat16)
    projected = jnp.einsum("hij,hc->ijc", tri_norm, w_out, preferred_element_type=jnp.float32)
    if ringed:
        split = projected.reshape(row_count, 2, chips, row_count, projected.shape[-1])
        projected = jnp.swapaxes(split, 1, 2).reshape(projected.shape)
    gating = jnp.einsum("ijc,cd->ijd", normed, w_out_gate, preferred_element_type=jnp.float32)
    return (jax.nn.sigmoid(gating) * projected).astype(jnp.bfloat16)


def solution(mesh):
    placed = (
        P(("groups", "row"), "sub", None),
        P("groups"),
        P(),
        P(None, "chan"),
        P(None, "chan"),
        P(None, "chan"),
        P(None, "chan"),
        P(),
        P(),
        P(),
    )
    return jax.shard_map(
        functools.partial(body, mesh.shape["row"], mesh.shape["chan"], mesh.shape["sub"]),
        mesh=mesh,
        in_specs=placed,
        out_specs=P(("groups", "row"), "sub", None),
        check_vma=False,
    )
```

```python
import functools

import jax
import jax.numpy as jnp
from jax import lax
from jax.experimental import pallas as pl
from jax.experimental.pallas import tpu as pltpu
from jax.sharding import PartitionSpec as P

MESH = pl.DeviceIdType.MESH


def norm_axis(values, gain, axis):
    mean = jnp.mean(values, axis=axis, keepdims=True)
    centered = values - mean
    variance = jnp.mean(centered * centered, axis=axis, keepdims=True)
    return centered * lax.rsqrt(variance + 1e-05) * gain


def ring_orders(chunks, half):
    orders = []
    for way in range(2):
        order = []
        for first in range(0, chunks, 2):
            pair = [q for q in (first, first + 1) if q < chunks]
            block = [(q, d) for d in range(1, half + 1) for q in pair]
            block = [(q, d) for q, d in block if d < half or q % 2 == way]
            if order:
                tail = order.pop()
                order += [block[0], tail] + block[1:]
            else:
                order = block
        orders.append(order)
    return orders


def triangle_kernel(
    chips,
    chunks,
    pair_ref,
    row_valid_ref,
    col_valid_ref,
    in_gain_ref,
    w_left_ref,
    w_left_gate_ref,
    w_right_ref,
    w_right_gate_ref,
    w_out_gate_ref,
    tri_ref,
    gate_ref,
    normed,
    weights,
    staged,
    held,
    lefts,
    part,
    sib_sem,
    ring_send,
    ring_recv,
    out_send,
    out_recv,
    local_sem,
):
    rows = pair_ref.shape[0]
    h_count = w_left_ref.shape[0]
    hc = h_count // chunks
    half = chips // 2
    index = lax.axis_index("row")
    x = lax.axis_index("chan")
    core = lax.rem(index, 2)
    chip = lax.div(index, 2)
    y = lax.rem(chip, 2)
    z = lax.div(chip, 2)
    place = jnp.where(y == 0, z, chips - 1 - z)

    def chip_at(ring_place):
        spot = lax.rem(ring_place + 2 * chips, chips)
        return jnp.where(spot < half, 2 * spot, 2 * (chips - 1 - spot) + 1)

    sibling = {"row": chip * 2 + (1 - core), "chan": x}
    nexts = [
        {"row": chip_at(place + 1) * 2 + core, "chan": x},
        {"row": chip_at(place - 1) * 2 + core, "chan": x},
    ]
    across = {"row": index, "chan": 1 - x}
    diagonal = {"row": chip * 2 + (1 - core), "chan": 1 - x}

    barrier = pltpu.get_barrier_semaphore()
    for partner in (sibling, nexts[0], nexts[1], across, diagonal):
        pl.semaphore_signal(barrier, inc=1, device_id=partner, device_id_type=MESH)

    def at_rows(block):
        return pl.ds(pl.multiple_of(block * rows, rows), rows)

    def at_heads(q):
        return pl.ds(q * hc, hc)

    weights[0, :h_count] = w_right_ref[...]
    weights[0, h_count:] = w_right_gate_ref[...]
    weights[1, :h_count] = w_left_ref[...]
    weights[1, h_count:] = w_left_gate_ref[...]
    col_valid = col_valid_ref[...].astype(jnp.float32)

    def project(i, side, block):
        both = lax.dot_general(
            weights[side], block, (((1,), (1,)), ((), ())), preferred_element_type=jnp.float32
        )
        weight = col_valid * row_valid_ref[index * rows + i].astype(jnp.float32)
        staged[side, i] = jax.nn.sigmoid(both[h_count:]) * both[:h_count] * weight

    def right_row(i, carry):
        values = pair_ref[i].astype(jnp.float32)
        mean = jnp.mean(values, axis=1, keepdims=True)
        centered = values - mean
        variance = jnp.mean(centered * centered, axis=1, keepdims=True)
        block = (centered * lax.rsqrt(variance + 1e-05) * in_gain_ref[...]).astype(jnp.bfloat16)
        normed[i] = block
        project(i, 0, block)
        return carry

    def left_row(i, carry):
        project(i, 1, normed[i])
        return carry

    def gate_row(i, carry):
        gate_ref[i] = jax.nn.sigmoid(
            jnp.dot(normed[i], w_out_gate_ref[...], preferred_element_type=jnp.float32)
        )
        return carry

    def turned(side, q):
        return jnp.swapaxes(staged[side, :, q * hc : (q + 1) * hc, :], 0, 1).astype(jnp.bfloat16)

    def turn_right(q):
        held[at_heads(q), at_rows(chip)] = turned(0, q)

    def ring_copy(way, q, d):
        step = 1 - 2 * way
        spot = held.at[at_heads(q), at_rows(chip_at(place - step * (d - 1)))]
        return pltpu.make_async_remote_copy(
            src_ref=spot,
            dst_ref=spot,
            send_sem=ring_send.at[way, q, d - 1],
            recv_sem=ring_recv.at[way, q, d - 1],
            device_id=nexts[way],
            device_id_type=MESH,
        )

    left_spot = lefts.at[:, at_rows(core)]
    left_copy = pltpu.make_async_remote_copy(
        src_ref=left_spot,
        dst_ref=left_spot,
        send_sem=sib_sem.at[0],
        recv_sem=sib_sem.at[1],
        device_id=sibling,
        device_id_type=MESH,
    )

    def send_left():
        for q in range(chunks):
            lefts[at_heads(q), at_rows(core)] = turned(1, q)
        left_copy.start()

    def out_copies(q):
        target = tri_ref.at[
            pl.ds(x * h_count + q * hc, hc), :, pl.ds(pl.multiple_of(core * rows * chips, 128), rows * chips)
        ]
        copies = []
        for n, (device, owner) in enumerate(((across, core), (diagonal, 1 - core), (sibling, 1 - core))):
            copies.append(
                pltpu.make_async_remote_copy(
                    src_ref=part.at[at_heads(q), at_rows(owner)],
                    dst_ref=target,
                    send_sem=out_send.at[n, q],
                    recv_sem=out_recv.at[n, q],
                    device_id=device,
                    device_id_type=MESH,
                )
            )
        own = pltpu.make_async_copy(part.at[at_heads(q), at_rows(core)], target, local_sem.at[q])
        return copies, own

    waited = set()

    def arrived(way, q, d):
        if (way, q, d) not in waited:
            ring_copy(way, q, d).wait_recv()
            waited.add((way, q, d))

    def compute(q):
        for way in range(2):
            top = half if q % 2 == way else half - 1
            for d in range(1, top + 1):
                arrived(way, q, d)
        heads = at_heads(q)
        product = lax.dot_general(
            lefts[heads], held[heads], (((2,), (2,)), ((0,), (0,))), preferred_element_type=jnp.float32
        )
        part[heads] = product.astype(jnp.bfloat16)
        copies, own = out_copies(q)
        for copy in copies:
            copy.start()
        own.start()

    lax.fori_loop(0, rows, right_row, 0)
    quarter = rows // 4
    tasks = [functools.partial(turn_right, q) for q in range(2, chunks)]
    tasks += [functools.partial(lax.fori_loop, n * quarter, (n + 1) * quarter, left_row, 0) for n in range(4)]
    tasks += [send_left]
    tasks += [functools.partial(lax.fori_loop, n * quarter, (n + 1) * quarter, gate_row, 0) for n in range(4)]

    orders = ring_orders(chunks, half)
    steps = len(orders[0])
    done = 0
    for n in range(steps):
        if n < 2:
            turn_right(n)
        if n == 0:
            pl.semaphore_wait(barrier, 5)
        for way in range(2):
            q, d = orders[way][n]
            if d > 1:
                arrived(way, q, d - 1)
            ring_copy(way, q, d).start()
        if n >= 1:
            for task in tasks[:2]:
                task()
            tasks = tasks[2:]
        last = max(orders[w].index((done, half if done % 2 == w else half - 1)) for w in range(2))
        if n >= last + 2 and n < steps - 1 and not tasks:
            if done == 0:
                left_copy.wait_recv()
            compute(done)
            done += 1
    for task in tasks:
        task()
    if done == 0:
        left_copy.wait_recv()
    while done < chunks:
        compute(done)
        done += 1
    for way in range(2):
        for q, d in orders[way]:
            ring_copy(way, q, d).wait_send()
    left_copy.wait_send()
    for q in range(chunks):
        copies, own = out_copies(q)
        for copy in copies:
            copy.wait()
        own.wait()


def triangle(chips, chunks, pair_act, residue_valid, in_gain, w_left, w_left_gate, w_right, w_right_gate, w_out_gate):
    rows, depth, channels = pair_act.shape
    h_count = w_left.shape[1]
    half = chips // 2
    dma = pltpu.SemaphoreType.DMA
    vmem = pl.BlockSpec(memory_space=pltpu.VMEM)
    smem = pl.BlockSpec(memory_space=pltpu.SMEM)
    return pl.pallas_call(
        functools.partial(triangle_kernel, chips, chunks),
        out_shape=[
            jax.ShapeDtypeStruct((2 * h_count, rows, chips * 2 * rows), jnp.bfloat16),
            jax.ShapeDtypeStruct((rows, depth, w_out_gate.shape[1]), jnp.float32),
        ],
        in_specs=[vmem, smem] + [vmem] * 7,
        out_specs=[vmem, vmem],
        scratch_shapes=[
            pltpu.VMEM((rows, depth, channels), jnp.bfloat16),
            pltpu.VMEM((2, 2 * h_count, channels), jnp.bfloat16),
            pltpu.VMEM((2, rows, h_count, depth), jnp.float32),
            pltpu.VMEM((h_count, chips * rows, depth), jnp.bfloat16),
            pltpu.VMEM((h_count, 2 * rows, depth), jnp.bfloat16),
            pltpu.VMEM((h_count, 2 * rows, chips * rows), jnp.bfloat16),
            dma((2,)),
            dma((2, chunks, half)),
            dma((2, chunks, half)),
            dma((3, chunks)),
            dma((3, chunks)),
            dma((chunks,)),
        ],
        compiler_params=pltpu.CompilerParams(
            collective_id=0, has_side_effects=True, vmem_limit_bytes=48 * 1024 * 1024
        ),
    )(
        pair_act,
        residue_valid,
        residue_valid[None, :],
        in_gain[None, :],
        w_left.T,
        w_left_gate.T,
        w_right.T,
        w_right_gate.T,
        w_out_gate,
    )


def finish(tri_full, out_gain, w_out):
    tri_norm = norm_axis(tri_full.astype(jnp.float32), out_gain[:, None, None], 0).astype(jnp.bfloat16)
    return jnp.einsum("hij,hc->ijc", tri_norm, w_out, preferred_element_type=jnp.float32)


def ring_body(chips, *operands):
    out_gain, w_out, w_out_gate = operands[-3:]
    tri_full, gate = triangle(chips, 4, *operands[:-3], w_out_gate)
    projected = finish(tri_full, out_gain, w_out)
    rows = operands[0].shape[0]
    split = projected.reshape(rows, 2, chips, rows, projected.shape[-1])
    return (gate * jnp.swapaxes(split, 1, 2).reshape(projected.shape)).astype(jnp.bfloat16)


def body(*operands):
    pair_act, residue_valid, in_gain, w_left, w_left_gate, w_right, w_right_gate, out_gain, w_out, w_out_gate = operands
    row_count = pair_act.shape[0]
    col_count = pair_act.shape[1]
    row_first = lax.axis_index("row") * row_count
    col_first = lax.axis_index("sub") * col_count
    normed = norm_axis(pair_act.astype(jnp.float32), in_gain, 2).astype(jnp.bfloat16)
    valid = residue_valid.astype(jnp.float32)
    row_valid = lax.dynamic_slice_in_dim(valid, row_first, row_count)
    col_valid = lax.dynamic_slice_in_dim(valid, col_first, col_count)
    weight = (row_valid[:, None] * col_valid[None, :])[None, :, :]

    def project(w_lin, w_gate):
        linear = jnp.einsum("ikc,ch->hik", normed, w_lin, preferred_element_type=jnp.float32)
        gating = jnp.einsum("ikc,ch->hik", normed, w_gate, preferred_element_type=jnp.float32)
        return (jax.nn.sigmoid(gating) * linear * weight).astype(jnp.bfloat16)

    left = project(w_left, w_left_gate)
    right = project(w_right, w_right_gate)
    right_all = lax.all_gather(right, "row", axis=1, tiled=True)
    partial_tri = lax.dot_general(
        left, right_all, (((2,), (2,)), ((0,), (0,))), preferred_element_type=jnp.float32
    )
    tri_half = lax.psum_scatter(partial_tri.astype(jnp.bfloat16), "sub", scatter_dimension=2, tiled=True)
    tri_full = lax.all_gather(tri_half, "chan", axis=0, tiled=True)
    gating = jnp.einsum("ijc,cd->ijd", normed, w_out_gate, preferred_element_type=jnp.float32)
    return (jax.nn.sigmoid(gating) * finish(tri_full, out_gain, w_out)).astype(jnp.bfloat16)


def solution(mesh):
    placed = (
        P(("groups", "row"), "sub", None),
        P("groups"),
        P(),
        P(None, "chan"),
        P(None, "chan"),
        P(None, "chan"),
        P(None, "chan"),
        P(),
        P(),
        P(),
    )
    rows, chan, sub = (mesh.shape[name] for name in ("row", "chan", "sub"))
    ringed = sub == 1 and chan == 2 and rows % 8 == 0
    return jax.shard_map(
        functools.partial(ring_body, rows // 2) if ringed else body,
        mesh=mesh,
        in_specs=placed,
        out_specs=P(("groups", "row"), "sub", None),
        check_vma=False,
    )
```

```python
import functools

import jax
import jax.numpy as jnp
from jax import lax
from jax.experimental import pallas as pl
from jax.experimental.pallas import tpu as pltpu
from jax.sharding import PartitionSpec as P

MESH = pl.DeviceIdType.MESH


def norm_axis(values, gain, axis):
    mean = jnp.mean(values, axis=axis, keepdims=True)
    centered = values - mean
    variance = jnp.mean(centered * centered, axis=axis, keepdims=True)
    return centered * lax.rsqrt(variance + 1e-05) * gain


def ring_orders(chunks, half):
    orders = []
    for way in range(2):
        order = []
        for first in range(0, chunks, 2):
            pair = [q for q in (first, first + 1) if q < chunks]
            block = [(q, d) for d in range(1, half + 1) for q in pair]
            block = [(q, d) for q, d in block if d < half or q % 2 == way]
            if order:
                tail = order.pop()
                order += [block[0], tail] + block[1:]
            else:
                order = block
        orders.append(order)
    return orders


def triangle_kernel(
    chips,
    chunks,
    row_valid_ref,
    pair_hbm,
    col_valid_hbm,
    in_gain_hbm,
    w_left_hbm,
    w_left_gate_hbm,
    w_right_hbm,
    w_right_gate_hbm,
    w_out_gate_hbm,
    tri_ref,
    gate_hbm,
    gate_ref,
    pair_ref,
    col_valid_ref,
    in_gain_ref,
    w_out_gate_ref,
    load_sem,
    normed,
    weights,
    staged,
    held,
    lefts,
    part,
    sib_sem,
    ring_send,
    ring_recv,
    out_send,
    out_recv,
    local_sem,
):
    rows = pair_hbm.shape[0]
    h_count = w_left_hbm.shape[0]
    hc = h_count // chunks
    half = chips // 2
    loads = [
        pltpu.make_async_copy(source, target, load_sem.at[n])
        for n, (source, target) in enumerate(
            (
                (pair_hbm, pair_ref),
                (in_gain_hbm, in_gain_ref),
                (col_valid_hbm, col_valid_ref),
                (w_right_hbm, weights.at[0, :h_count]),
                (w_right_gate_hbm, weights.at[0, h_count:]),
                (w_left_hbm, weights.at[1, :h_count]),
                (w_left_gate_hbm, weights.at[1, h_count:]),
                (w_out_gate_hbm, w_out_gate_ref),
            )
        )
    ]
    for load in loads:
        load.start()
    index = lax.axis_index("row")
    x = lax.axis_index("chan")
    core = lax.rem(index, 2)
    chip = lax.div(index, 2)
    y = lax.rem(chip, 2)
    z = lax.div(chip, 2)
    place = jnp.where(y == 0, z, chips - 1 - z)

    def chip_at(ring_place):
        spot = lax.rem(ring_place + 2 * chips, chips)
        return jnp.where(spot < half, 2 * spot, 2 * (chips - 1 - spot) + 1)

    sibling = {"row": chip * 2 + (1 - core), "chan": x}
    nexts = [
        {"row": chip_at(place + 1) * 2 + core, "chan": x},
        {"row": chip_at(place - 1) * 2 + core, "chan": x},
    ]
    across = {"row": index, "chan": 1 - x}
    diagonal = {"row": chip * 2 + (1 - core), "chan": 1 - x}

    barrier = pltpu.get_barrier_semaphore()
    for partner in (sibling, nexts[0], nexts[1], across, diagonal):
        pl.semaphore_signal(barrier, inc=1, device_id=partner, device_id_type=MESH)

    def at_rows(block):
        return pl.ds(pl.multiple_of(block * rows, rows), rows)

    def at_heads(q):
        return pl.ds(q * hc, hc)

    for load in loads:
        load.wait()
    col_valid = col_valid_ref[...].astype(jnp.float32)

    def project(i, side, block):
        both = lax.dot_general(
            weights[side], block, (((1,), (1,)), ((), ())), preferred_element_type=jnp.float32
        )
        weight = col_valid * row_valid_ref[index * rows + i].astype(jnp.float32)
        staged[side, i] = jax.nn.sigmoid(both[h_count:]) * both[:h_count] * weight

    def right_row(i, carry):
        values = pair_ref[i].astype(jnp.float32)
        mean = jnp.mean(values, axis=1, keepdims=True)
        centered = values - mean
        variance = jnp.mean(centered * centered, axis=1, keepdims=True)
        block = (centered * lax.rsqrt(variance + 1e-05) * in_gain_ref[...]).astype(jnp.bfloat16)
        normed[i] = block
        project(i, 0, block)
        return carry

    def left_row(i, carry):
        project(i, 1, normed[i])
        return carry

    def gate_row(i, carry):
        gate_ref[i] = jax.nn.sigmoid(
            jnp.dot(normed[i], w_out_gate_ref[...], preferred_element_type=jnp.float32)
        )
        return carry

    def turned(side, q):
        return jnp.swapaxes(staged[side, :, q * hc : (q + 1) * hc, :], 0, 1).astype(jnp.bfloat16)

    def turn_right(q):
        held[at_heads(q), at_rows(chip)] = turned(0, q)

    def ring_copy(way, q, d):
        step = 1 - 2 * way
        spot = held.at[at_heads(q), at_rows(chip_at(place - step * (d - 1)))]
        return pltpu.make_async_remote_copy(
            src_ref=spot,
            dst_ref=spot,
            send_sem=ring_send.at[way, q, d - 1],
            recv_sem=ring_recv.at[way, q, d - 1],
            device_id=nexts[way],
            device_id_type=MESH,
        )

    left_spot = lefts.at[:, at_rows(core)]
    left_copy = pltpu.make_async_remote_copy(
        src_ref=left_spot,
        dst_ref=left_spot,
        send_sem=sib_sem.at[0],
        recv_sem=sib_sem.at[1],
        device_id=sibling,
        device_id_type=MESH,
    )

    def send_left():
        for q in range(chunks):
            lefts[at_heads(q), at_rows(core)] = turned(1, q)
        left_copy.start()

    def out_copies(q):
        target = tri_ref.at[
            pl.ds(x * h_count + q * hc, hc), :, pl.ds(pl.multiple_of(core * rows * chips, 128), rows * chips)
        ]
        copies = []
        for n, (device, owner) in enumerate(((across, core), (diagonal, 1 - core), (sibling, 1 - core))):
            copies.append(
                pltpu.make_async_remote_copy(
                    src_ref=part.at[at_heads(q), at_rows(owner)],
                    dst_ref=target,
                    send_sem=out_send.at[n, q],
                    recv_sem=out_recv.at[n, q],
                    device_id=device,
                    device_id_type=MESH,
                )
            )
        own = pltpu.make_async_copy(part.at[at_heads(q), at_rows(core)], target, local_sem.at[q])
        return copies, own

    waited = set()

    def arrived(way, q, d):
        if (way, q, d) not in waited:
            ring_copy(way, q, d).wait_recv()
            waited.add((way, q, d))

    def compute(q):
        for way in range(2):
            top = half if q % 2 == way else half - 1
            for d in range(1, top + 1):
                arrived(way, q, d)
        heads = at_heads(q)
        product = lax.dot_general(
            lefts[heads], held[heads], (((2,), (2,)), ((0,), (0,))), preferred_element_type=jnp.float32
        )
        part[heads] = product.astype(jnp.bfloat16)
        copies, own = out_copies(q)
        for copy in copies:
            copy.start()
        own.start()

    gate_copy = pltpu.make_async_copy(gate_ref, gate_hbm, load_sem.at[8])
    lax.fori_loop(0, rows, right_row, 0)
    quarter = rows // 4
    tasks = [functools.partial(turn_right, q) for q in range(2, chunks)]
    tasks += [functools.partial(lax.fori_loop, n * quarter, (n + 1) * quarter, left_row, 0) for n in range(4)]
    tasks += [send_left]
    tasks += [functools.partial(lax.fori_loop, n * quarter, (n + 1) * quarter, gate_row, 0) for n in range(4)]
    tasks += [gate_copy.start]

    orders = ring_orders(chunks, half)
    steps = len(orders[0])
    done = 0
    for n in range(steps):
        if n < 2:
            turn_right(n)
        if n == 0:
            pl.semaphore_wait(barrier, 5)
        for way in range(2):
            q, d = orders[way][n]
            if d > 1:
                arrived(way, q, d - 1)
            ring_copy(way, q, d).start()
        if n >= 1:
            for task in tasks[:2]:
                task()
            tasks = tasks[2:]
        last = max(orders[w].index((done, half if done % 2 == w else half - 1)) for w in range(2))
        if n >= last + 2 and n < steps - 1 and not tasks:
            if done == 0:
                left_copy.wait_recv()
            compute(done)
            done += 1
    for task in tasks:
        task()
    if done == 0:
        left_copy.wait_recv()
    while done < chunks:
        compute(done)
        done += 1
    for way in range(2):
        for q, d in orders[way]:
            ring_copy(way, q, d).wait_send()
    left_copy.wait_send()
    gate_copy.wait()
    for q in range(chunks):
        copies, own = out_copies(q)
        for copy in copies:
            copy.wait()
        own.wait()


def triangle(chips, chunks, pair_act, residue_valid, in_gain, w_left, w_left_gate, w_right, w_right_gate, w_out_gate):
    rows, depth, channels = pair_act.shape
    h_count = w_left.shape[1]
    half = chips // 2
    dma = pltpu.SemaphoreType.DMA
    vmem = pl.BlockSpec(memory_space=pltpu.VMEM)
    smem = pl.BlockSpec(memory_space=pltpu.SMEM)
    return pl.pallas_call(
        functools.partial(triangle_kernel, chips, chunks),
        out_shape=[
            jax.ShapeDtypeStruct((2 * h_count, rows, chips * 2 * rows), jnp.bfloat16),
            jax.ShapeDtypeStruct((rows, depth, w_out_gate.shape[1]), jnp.float32),
        ],
        in_specs=[smem] + [pl.BlockSpec(memory_space=pltpu.HBM)] * 8,
        out_specs=[vmem, pl.BlockSpec(memory_space=pltpu.HBM)],
        scratch_shapes=[
            pltpu.VMEM((rows, depth, w_out_gate.shape[1]), jnp.float32),
            pltpu.VMEM((rows, depth, channels), jnp.bfloat16),
            pltpu.VMEM((1, depth), jnp.int32),
            pltpu.VMEM((1, channels), jnp.float32),
            pltpu.VMEM(w_out_gate.shape, jnp.bfloat16),
            dma((9,)),
            pltpu.VMEM((rows, depth, channels), jnp.bfloat16),
            pltpu.VMEM((2, 2 * h_count, channels), jnp.bfloat16),
            pltpu.VMEM((2, rows, h_count, depth), jnp.float32),
            pltpu.VMEM((h_count, chips * rows, depth), jnp.bfloat16),
            pltpu.VMEM((h_count, 2 * rows, depth), jnp.bfloat16),
            pltpu.VMEM((h_count, 2 * rows, chips * rows), jnp.bfloat16),
            dma((2,)),
            dma((2, chunks, half)),
            dma((2, chunks, half)),
            dma((3, chunks)),
            dma((3, chunks)),
            dma((chunks,)),
        ],
        compiler_params=pltpu.CompilerParams(
            collective_id=0, has_side_effects=True, vmem_limit_bytes=60 * 1024 * 1024
        ),
    )(
        residue_valid,
        pair_act,
        residue_valid[None, :],
        in_gain[None, :],
        w_left.T,
        w_left_gate.T,
        w_right.T,
        w_right_gate.T,
        w_out_gate,
    )


def finish(tri_full, out_gain, w_out):
    tri_norm = norm_axis(tri_full.astype(jnp.float32), out_gain[:, None, None], 0).astype(jnp.bfloat16)
    return jnp.einsum("hij,hc->ijc", tri_norm, w_out, preferred_element_type=jnp.float32)


def ring_body(chips, *operands):
    out_gain, w_out, w_out_gate = operands[-3:]
    tri_full, gate = triangle(chips, 4, *operands[:-3], w_out_gate)
    projected = finish(tri_full, out_gain, w_out)
    rows = operands[0].shape[0]
    split = projected.reshape(rows, 2, chips, rows, projected.shape[-1])
    return (gate * jnp.swapaxes(split, 1, 2).reshape(projected.shape)).astype(jnp.bfloat16)


def body(*operands):
    pair_act, residue_valid, in_gain, w_left, w_left_gate, w_right, w_right_gate, out_gain, w_out, w_out_gate = operands
    row_count = pair_act.shape[0]
    col_count = pair_act.shape[1]
    row_first = lax.axis_index("row") * row_count
    col_first = lax.axis_index("sub") * col_count
    normed = norm_axis(pair_act.astype(jnp.float32), in_gain, 2).astype(jnp.bfloat16)
    valid = residue_valid.astype(jnp.float32)
    row_valid = lax.dynamic_slice_in_dim(valid, row_first, row_count)
    col_valid = lax.dynamic_slice_in_dim(valid, col_first, col_count)
    weight = (row_valid[:, None] * col_valid[None, :])[None, :, :]

    def project(w_lin, w_gate):
        linear = jnp.einsum("ikc,ch->hik", normed, w_lin, preferred_element_type=jnp.float32)
        gating = jnp.einsum("ikc,ch->hik", normed, w_gate, preferred_element_type=jnp.float32)
        return (jax.nn.sigmoid(gating) * linear * weight).astype(jnp.bfloat16)

    left = project(w_left, w_left_gate)
    right = project(w_right, w_right_gate)
    right_all = lax.all_gather(right, "row", axis=1, tiled=True)
    partial_tri = lax.dot_general(
        left, right_all, (((2,), (2,)), ((0,), (0,))), preferred_element_type=jnp.float32
    )
    tri_half = lax.psum_scatter(partial_tri.astype(jnp.bfloat16), "sub", scatter_dimension=2, tiled=True)
    tri_full = lax.all_gather(tri_half, "chan", axis=0, tiled=True)
    gating = jnp.einsum("ijc,cd->ijd", normed, w_out_gate, preferred_element_type=jnp.float32)
    return (jax.nn.sigmoid(gating) * finish(tri_full, out_gain, w_out)).astype(jnp.bfloat16)


def solution(mesh):
    placed = (
        P(("groups", "row"), "sub", None),
        P("groups"),
        P(),
        P(None, "chan"),
        P(None, "chan"),
        P(None, "chan"),
        P(None, "chan"),
        P(),
        P(),
        P(),
    )
    rows, chan, sub = (mesh.shape[name] for name in ("row", "chan", "sub"))
    ringed = sub == 1 and chan == 2 and rows % 8 == 0
    return jax.shard_map(
        functools.partial(ring_body, rows // 2) if ringed else body,
        mesh=mesh,
        in_specs=placed,
        out_specs=P(("groups", "row"), "sub", None),
        check_vma=False,
    )
```

```python
import functools

import jax
import jax.numpy as jnp
from jax import lax
from jax.experimental import pallas as pl
from jax.experimental.pallas import tpu as pltpu
from jax.sharding import PartitionSpec as P

CHUNKS = 4
MESH = pl.DeviceIdType.MESH


def norm_axis(values, gain, axis):
    mean = jnp.mean(values, axis=axis, keepdims=True)
    centered = values - mean
    variance = jnp.mean(centered * centered, axis=axis, keepdims=True)
    return centered * lax.rsqrt(variance + 1e-05) * gain


def ring_orders(chunks, half):
    orders = []
    for way in range(2):
        order = []
        for first in range(0, chunks, 2):
            pair = [q for q in (first, first + 1) if q < chunks]
            block = [(q, d) for d in range(1, half + 1) for q in pair]
            block = [(q, d) for q, d in block if d < half or q % 2 == way]
            if order:
                tail = order.pop()
                order += [block[0], tail] + block[1:]
            else:
                order = block
        orders.append(order)
    return orders


def triangle_kernel(
    chips,
    chunks,
    row_valid_ref,
    pair_hbm,
    col_valid_hbm,
    in_gain_hbm,
    w_left_hbm,
    w_left_gate_hbm,
    w_right_hbm,
    w_right_gate_hbm,
    w_out_gate_hbm,
    out_gain_hbm,
    w_out_hbm,
    update_ref,
    tri_ref,
    by_row,
    gate_ref,
    out_gain_ref,
    gain_columns,
    w_out_ref,
    pair_ref,
    col_valid_ref,
    in_gain_ref,
    w_out_gate_ref,
    load_sem,
    normed,
    weights,
    staged,
    held,
    lefts,
    part,
    sib_sem,
    ring_send,
    ring_recv,
    out_send,
    out_recv,
    local_sem,
):
    rows = pair_hbm.shape[0]
    h_count = w_left_hbm.shape[0]
    hc = h_count // chunks
    half = chips // 2
    loads = [
        pltpu.make_async_copy(source, target, load_sem.at[n])
        for n, (source, target) in enumerate(
            (
                (pair_hbm, pair_ref),
                (in_gain_hbm, in_gain_ref),
                (col_valid_hbm, col_valid_ref),
                (w_right_hbm, weights.at[0, :h_count]),
                (w_right_gate_hbm, weights.at[0, h_count:]),
                (w_left_hbm, weights.at[1, :h_count]),
                (w_left_gate_hbm, weights.at[1, h_count:]),
                (w_out_gate_hbm, w_out_gate_ref),
                (out_gain_hbm, out_gain_ref),
                (w_out_hbm, w_out_ref),
            )
        )
    ]
    for load in loads:
        load.start()
    index = lax.axis_index("row")
    x = lax.axis_index("chan")
    core = lax.rem(index, 2)
    chip = lax.div(index, 2)
    y = lax.rem(chip, 2)
    z = lax.div(chip, 2)
    place = jnp.where(y == 0, z, chips - 1 - z)

    def chip_at(ring_place):
        spot = lax.rem(ring_place + 2 * chips, chips)
        return jnp.where(spot < half, 2 * spot, 2 * (chips - 1 - spot) + 1)

    sibling = {"row": chip * 2 + (1 - core), "chan": x}
    nexts = [
        {"row": chip_at(place + 1) * 2 + core, "chan": x},
        {"row": chip_at(place - 1) * 2 + core, "chan": x},
    ]
    across = {"row": index, "chan": 1 - x}
    diagonal = {"row": chip * 2 + (1 - core), "chan": 1 - x}

    barrier = pltpu.get_barrier_semaphore()
    for partner in (sibling, nexts[0], nexts[1], across, diagonal):
        pl.semaphore_signal(barrier, inc=1, device_id=partner, device_id_type=MESH)

    def at_rows(block):
        return pl.ds(pl.multiple_of(block * rows, rows), rows)

    def at_heads(q):
        return pl.ds(q * hc, hc)

    for load in loads:
        load.wait()
    col_valid = col_valid_ref[...].astype(jnp.float32)

    def project(i, side, block):
        both = lax.dot_general(
            weights[side], block, (((1,), (1,)), ((), ())), preferred_element_type=jnp.float32
        )
        weight = col_valid * row_valid_ref[index * rows + i].astype(jnp.float32)
        staged[side, i] = jax.nn.sigmoid(both[h_count:]) * both[:h_count] * weight

    def right_row(i, carry):
        values = pair_ref[i].astype(jnp.float32)
        mean = jnp.mean(values, axis=1, keepdims=True)
        centered = values - mean
        variance = jnp.mean(centered * centered, axis=1, keepdims=True)
        block = (centered * lax.rsqrt(variance + 1e-05) * in_gain_ref[...]).astype(jnp.bfloat16)
        normed[i] = block
        project(i, 0, block)
        return carry

    def left_row(i, carry):
        project(i, 1, normed[i])
        return carry

    def gate_row(i, carry):
        gate_ref[i] = jax.nn.sigmoid(
            jnp.dot(normed[i], w_out_gate_ref[...], preferred_element_type=jnp.float32)
        )
        return carry

    def turned(side, q):
        return jnp.swapaxes(staged[side, :, q * hc : (q + 1) * hc, :], 0, 1).astype(jnp.bfloat16)

    def turn_right(q):
        held[at_heads(q), at_rows(chip)] = turned(0, q)

    def ring_copy(way, q, d):
        step = 1 - 2 * way
        spot = held.at[at_heads(q), at_rows(chip_at(place - step * (d - 1)))]
        return pltpu.make_async_remote_copy(
            src_ref=spot,
            dst_ref=spot,
            send_sem=ring_send.at[way, q, d - 1],
            recv_sem=ring_recv.at[way, q, d - 1],
            device_id=nexts[way],
            device_id_type=MESH,
        )

    left_spot = lefts.at[:, at_rows(core)]
    left_copy = pltpu.make_async_remote_copy(
        src_ref=left_spot,
        dst_ref=left_spot,
        send_sem=sib_sem.at[0],
        recv_sem=sib_sem.at[1],
        device_id=sibling,
        device_id_type=MESH,
    )

    def send_left():
        for q in range(chunks):
            lefts[at_heads(q), at_rows(core)] = turned(1, q)
        left_copy.start()

    def out_copies(q):
        target = tri_ref.at[
            pl.ds(x * h_count + q * hc, hc), :, pl.ds(pl.multiple_of(core * rows * chips, 128), rows * chips)
        ]
        copies = []
        for n, (device, owner) in enumerate(((across, core), (diagonal, 1 - core), (sibling, 1 - core))):
            copies.append(
                pltpu.make_async_remote_copy(
                    src_ref=part.at[at_heads(q), at_rows(owner)],
                    dst_ref=target,
                    send_sem=out_send.at[n, q],
                    recv_sem=out_recv.at[n, q],
                    device_id=device,
                    device_id_type=MESH,
                )
            )
        own = pltpu.make_async_copy(part.at[at_heads(q), at_rows(core)], target, local_sem.at[q])
        return copies, own

    def collect(q):
        copies, own = out_copies(q)
        for copy in copies:
            copy.wait_recv()
        own.wait()
        for side in range(2):
            first = side * h_count + q * hc
            by_row[:, first : first + hc, :] = jnp.swapaxes(
                tri_ref[first : first + hc].astype(jnp.float32), 0, 1
            )

    def finish_row(i, carry):
        values = by_row[i]
        mean = jnp.mean(values, axis=0, keepdims=True)
        centered = values - mean
        variance = jnp.mean(centered * centered, axis=0, keepdims=True)
        block = (centered * lax.rsqrt(variance + 1e-05) * gain_columns[:, :1]).astype(jnp.bfloat16)
        projected = lax.dot_general(
            block, w_out_ref[...], (((0,), (0,)), ((), ())), preferred_element_type=jnp.float32
        )
        for other in range(2):
            for there in range(chips):
                source = (other * chips + there) * rows
                target = pl.ds((there * 2 + other) * rows, rows)
                update_ref[i, target, :] = (
                    gate_ref[i, target, :] * projected[source : source + rows]
                ).astype(jnp.bfloat16)
        return carry

    waited = set()

    def arrived(way, q, d):
        if (way, q, d) not in waited:
            ring_copy(way, q, d).wait_recv()
            waited.add((way, q, d))

    def compute(q):
        for way in range(2):
            top = half if q % 2 == way else half - 1
            for d in range(1, top + 1):
                arrived(way, q, d)
        heads = at_heads(q)
        product = lax.dot_general(
            lefts[heads], held[heads], (((2,), (2,)), ((0,), (0,))), preferred_element_type=jnp.float32
        )
        part[heads] = product.astype(jnp.bfloat16)
        copies, own = out_copies(q)
        for copy in copies:
            copy.start()
        own.start()

    lax.fori_loop(0, rows, right_row, 0, unroll=2)
    gain_columns[...] = jnp.swapaxes(jnp.broadcast_to(out_gain_ref[...], gain_columns.shape), 0, 1)
    quarter = rows // 4
    tasks = [functools.partial(turn_right, q) for q in range(2, chunks)]
    tasks += [functools.partial(lax.fori_loop, n * quarter, (n + 1) * quarter, left_row, 0) for n in range(4)]
    tasks += [send_left]
    tasks += [functools.partial(lax.fori_loop, n * quarter, (n + 1) * quarter, gate_row, 0) for n in range(4)]

    orders = ring_orders(chunks, half)
    steps = len(orders[0])
    done = 0
    for n in range(steps):
        if n < 2:
            turn_right(n)
        if n == 0:
            pl.semaphore_wait(barrier, 5)
        for way in range(2):
            q, d = orders[way][n]
            if d > 1:
                arrived(way, q, d - 1)
            ring_copy(way, q, d).start()
        if n >= 1:
            for task in tasks[:2]:
                task()
            tasks = tasks[2:]
        last = max(orders[w].index((done, half if done % 2 == w else half - 1)) for w in range(2))
        if n >= last + 2 and n < steps - 1 and not tasks:
            if done == 0:
                left_copy.wait_recv()
            compute(done)
            if done:
                collect(done - 1)
            done += 1
    for task in tasks:
        task()
    if done == 0:
        left_copy.wait_recv()
    while done < chunks:
        compute(done)
        if done:
            collect(done - 1)
        done += 1
    collect(chunks - 1)
    lax.fori_loop(0, rows, finish_row, 0, unroll=2)
    for way in range(2):
        for q, d in orders[way]:
            ring_copy(way, q, d).wait_send()
    left_copy.wait_send()
    for q in range(chunks):
        for copy in out_copies(q)[0]:
            copy.wait_send()


def triangle(chips, chunks, pair_act, residue_valid, in_gain, w_left, w_left_gate, w_right, w_right_gate, out_gain, w_out, w_out_gate):
    rows, depth, channels = pair_act.shape
    h_count = w_left.shape[1]
    half = chips // 2
    dma = pltpu.SemaphoreType.DMA
    vmem = pl.BlockSpec(memory_space=pltpu.VMEM)
    smem = pl.BlockSpec(memory_space=pltpu.SMEM)
    return pl.pallas_call(
        functools.partial(triangle_kernel, chips, chunks),
        out_shape=jax.ShapeDtypeStruct((rows, depth, w_out.shape[1]), jnp.bfloat16),
        in_specs=[smem] + [pl.BlockSpec(memory_space=pltpu.HBM)] * 10,
        out_specs=vmem,
        scratch_shapes=[
            pltpu.VMEM((2 * h_count, rows, chips * 2 * rows), jnp.bfloat16),
            pltpu.VMEM((rows, 2 * h_count, chips * 2 * rows), jnp.float32),
            pltpu.VMEM((rows, depth, w_out_gate.shape[1]), jnp.float32),
            pltpu.VMEM((1, 2 * h_count), jnp.float32),
            pltpu.VMEM((2 * h_count, 2 * h_count), jnp.float32),
            pltpu.VMEM(w_out.shape, jnp.bfloat16),
            pltpu.VMEM((rows, depth, channels), jnp.bfloat16),
            pltpu.VMEM((1, depth), jnp.int32),
            pltpu.VMEM((1, channels), jnp.float32),
            pltpu.VMEM(w_out_gate.shape, jnp.bfloat16),
            dma((10,)),
            pltpu.VMEM((rows, depth, channels), jnp.bfloat16),
            pltpu.VMEM((2, 2 * h_count, channels), jnp.bfloat16),
            pltpu.VMEM((2, rows, h_count, depth), jnp.float32),
            pltpu.VMEM((h_count, chips * rows, depth), jnp.bfloat16),
            pltpu.VMEM((h_count, 2 * rows, depth), jnp.bfloat16),
            pltpu.VMEM((h_count, 2 * rows, chips * rows), jnp.bfloat16),
            dma((2,)),
            dma((2, chunks, half)),
            dma((2, chunks, half)),
            dma((3, chunks)),
            dma((3, chunks)),
            dma((chunks,)),
        ],
        compiler_params=pltpu.CompilerParams(
            collective_id=0, has_side_effects=True, vmem_limit_bytes=60 * 1024 * 1024
        ),
    )(
        residue_valid,
        pair_act,
        residue_valid[None, :],
        in_gain[None, :],
        w_left.T,
        w_left_gate.T,
        w_right.T,
        w_right_gate.T,
        w_out_gate,
        out_gain[None, :],
        w_out,
    )


def finish(tri_full, out_gain, w_out):
    tri_norm = norm_axis(tri_full.astype(jnp.float32), out_gain[:, None, None], 0).astype(jnp.bfloat16)
    return jnp.einsum("hij,hc->ijc", tri_norm, w_out, preferred_element_type=jnp.float32)


def ring_body(chips, *operands):
    return triangle(chips, CHUNKS, *operands)


def body(*operands):
    pair_act, residue_valid, in_gain, w_left, w_left_gate, w_right, w_right_gate, out_gain, w_out, w_out_gate = operands
    row_count = pair_act.shape[0]
    col_count = pair_act.shape[1]
    row_first = lax.axis_index("row") * row_count
    col_first = lax.axis_index("sub") * col_count
    normed = norm_axis(pair_act.astype(jnp.float32), in_gain, 2).astype(jnp.bfloat16)
    valid = residue_valid.astype(jnp.float32)
    row_valid = lax.dynamic_slice_in_dim(valid, row_first, row_count)
    col_valid = lax.dynamic_slice_in_dim(valid, col_first, col_count)
    weight = (row_valid[:, None] * col_valid[None, :])[None, :, :]

    def project(w_lin, w_gate):
        linear = jnp.einsum("ikc,ch->hik", normed, w_lin, preferred_element_type=jnp.float32)
        gating = jnp.einsum("ikc,ch->hik", normed, w_gate, preferred_element_type=jnp.float32)
        return (jax.nn.sigmoid(gating) * linear * weight).astype(jnp.bfloat16)

    left = project(w_left, w_left_gate)
    right = project(w_right, w_right_gate)
    right_all = lax.all_gather(right, "row", axis=1, tiled=True)
    partial_tri = lax.dot_general(
        left, right_all, (((2,), (2,)), ((0,), (0,))), preferred_element_type=jnp.float32
    )
    tri_half = lax.psum_scatter(partial_tri.astype(jnp.bfloat16), "sub", scatter_dimension=2, tiled=True)
    tri_full = lax.all_gather(tri_half, "chan", axis=0, tiled=True)
    gating = jnp.einsum("ijc,cd->ijd", normed, w_out_gate, preferred_element_type=jnp.float32)
    return (jax.nn.sigmoid(gating) * finish(tri_full, out_gain, w_out)).astype(jnp.bfloat16)


def solution(mesh):
    placed = (
        P(("groups", "row"), "sub", None),
        P("groups"),
        P(),
        P(None, "chan"),
        P(None, "chan"),
        P(None, "chan"),
        P(None, "chan"),
        P(),
        P(),
        P(),
    )
    rows, chan, sub = (mesh.shape[name] for name in ("row", "chan", "sub"))
    ringed = sub == 1 and chan == 2 and rows % 8 == 0
    return jax.shard_map(
        functools.partial(ring_body, rows // 2) if ringed else body,
        mesh=mesh,
        in_specs=placed,
        out_specs=P(("groups", "row"), "sub", None),
        check_vma=False,
    )
```

```python
import functools

import jax
import jax.numpy as jnp
from jax import lax
from jax.experimental import pallas as pl
from jax.experimental.pallas import tpu as pltpu
from jax.sharding import PartitionSpec as P

CHUNKS = 4
MESH = pl.DeviceIdType.MESH


def norm_axis(values, gain, axis):
    mean = jnp.mean(values, axis=axis, keepdims=True)
    centered = values - mean
    variance = jnp.mean(centered * centered, axis=axis, keepdims=True)
    return centered * lax.rsqrt(variance + 1e-05) * gain


def line_order(chunks, reach):
    order = []
    for first in range(0, chunks, 2):
        pair = [q for q in (first, first + 1) if q < chunks]
        block = [(q, d) for d in range(1, reach + 1) for q in pair]
        if order:
            tail = order.pop()
            order += [block[0], tail] + block[1:]
        else:
            order = block
    return order


def triangle_kernel(
    chips,
    chunks,
    row_valid_ref,
    pair_hbm,
    col_valid_hbm,
    in_gain_hbm,
    w_left_hbm,
    w_left_gate_hbm,
    w_right_hbm,
    w_right_gate_hbm,
    w_out_gate_hbm,
    out_gain_hbm,
    w_out_hbm,
    update_ref,
    tri_ref,
    by_row,
    gate_ref,
    out_gain_ref,
    gain_columns,
    w_out_ref,
    pair_ref,
    col_valid_ref,
    in_gain_ref,
    w_out_gate_ref,
    load_sem,
    normed,
    weights,
    staged,
    held,
    lefts,
    part,
    sib_sem,
    ring_send,
    ring_recv,
    pair_send,
    pair_recv,
    out_send,
    out_recv,
    local_sem,
):
    rows = pair_hbm.shape[0]
    h_count = w_left_hbm.shape[0]
    hc = h_count // chunks
    half = chips // 2
    loads = [
        pltpu.make_async_copy(source, target, load_sem.at[n])
        for n, (source, target) in enumerate(
            (
                (pair_hbm, pair_ref),
                (in_gain_hbm, in_gain_ref),
                (col_valid_hbm, col_valid_ref),
                (w_right_hbm, weights.at[0, :h_count]),
                (w_right_gate_hbm, weights.at[0, h_count:]),
                (w_left_hbm, weights.at[1, :h_count]),
                (w_left_gate_hbm, weights.at[1, h_count:]),
                (w_out_gate_hbm, w_out_gate_ref),
                (out_gain_hbm, out_gain_ref),
                (w_out_hbm, w_out_ref),
            )
        )
    ]
    for load in loads:
        load.start()
    index = lax.axis_index("row")
    x = lax.axis_index("chan")
    core = lax.rem(index, 2)
    chip = lax.div(index, 2)
    y = lax.rem(chip, 2)
    z = lax.div(chip, 2)
    reach = half - 1
    sibling = {"row": chip * 2 + (1 - core), "chan": x}
    nexts = [{"row": index + 4, "chan": x}, {"row": index - 4, "chan": x}]
    has_next = [z < half - 1, z > 0]
    beside = {"row": (2 * z + 1 - y) * 2 + core, "chan": x}
    across = {"row": index, "chan": 1 - x}
    diagonal = {"row": (2 * z + 1 - y) * 2 + core, "chan": 1 - x}

    barrier = pltpu.get_barrier_semaphore()
    for partner in (sibling, beside, across, diagonal):
        pl.semaphore_signal(barrier, inc=1, device_id=partner, device_id_type=MESH)
    for way in range(2):

        @pl.when(has_next[way])
        def _():
            pl.semaphore_signal(barrier, inc=1, device_id=nexts[way], device_id_type=MESH)

    partners = 4 + jnp.where(z < half - 1, 1, 0) + jnp.where(z > 0, 1, 0)

    def at_rows(block):
        return pl.ds(pl.multiple_of(block * rows, rows), rows)

    def at_heads(q):
        return pl.ds(q * hc, hc)

    for load in loads:
        load.wait()
    col_valid = col_valid_ref[...].astype(jnp.float32)

    def project(i, side, block):
        both = lax.dot_general(
            weights[side], block, (((1,), (1,)), ((), ())), preferred_element_type=jnp.float32
        )
        weight = col_valid * row_valid_ref[index * rows + i].astype(jnp.float32)
        staged[side, i] = jax.nn.sigmoid(both[h_count:]) * both[:h_count] * weight

    def right_row(i, carry):
        values = pair_ref[i].astype(jnp.float32)
        mean = jnp.mean(values, axis=1, keepdims=True)
        centered = values - mean
        variance = jnp.mean(centered * centered, axis=1, keepdims=True)
        block = (centered * lax.rsqrt(variance + 1e-05) * in_gain_ref[...]).astype(jnp.bfloat16)
        normed[i] = block
        project(i, 0, block)
        return carry

    def left_row(i, carry):
        project(i, 1, normed[i])
        return carry

    def gate_row(i, carry):
        gate_ref[i] = jax.nn.sigmoid(
            jnp.dot(normed[i], w_out_gate_ref[...], preferred_element_type=jnp.float32)
        )
        return carry

    def turned(side, q):
        return jnp.swapaxes(staged[side, :, q * hc : (q + 1) * hc, :], 0, 1).astype(jnp.bfloat16)

    def turn_right(q):
        held[at_heads(q), at_rows(2 * z + core)] = turned(0, q)


    def origin(way, d):
        return z - (1 - 2 * way) * d

    def exists(way, d):
        return origin(way, d) >= 0 if way == 0 else origin(way, d) < half

    def ring_copy(way, q, d):
        spot = held.at[at_heads(q), at_rows(2 * origin(way, d - 1) + core)]
        return pltpu.make_async_remote_copy(
            src_ref=spot,
            dst_ref=spot,
            send_sem=ring_send.at[way, q, d - 1],
            recv_sem=ring_recv.at[way, q, d - 1],
            device_id=nexts[way],
            device_id_type=MESH,
        )

    def sibling_copy(way, q, d):
        spot = held.at[at_heads(q), at_rows(2 * origin(way, d) + core)]
        return pltpu.make_async_remote_copy(
            src_ref=spot,
            dst_ref=spot,
            send_sem=pair_send.at[way, q, d],
            recv_sem=pair_recv.at[way, q, d],
            device_id=sibling,
            device_id_type=MESH,
        )

    def each_piece(q, act):
        act(sibling_copy(0, q, 0))
        for way in range(2):
            for d in range(1, reach + 1):

                @pl.when(exists(way, d))
                def _():
                    act(sibling_copy(way, q, d))

    left_spot = lefts.at[:, at_rows(y)]
    left_copy = pltpu.make_async_remote_copy(
        src_ref=left_spot,
        dst_ref=left_spot,
        send_sem=sib_sem.at[0],
        recv_sem=sib_sem.at[1],
        device_id=beside,
        device_id_type=MESH,
    )

    def send_left():
        for q in range(chunks):
            lefts[at_heads(q), at_rows(y)] = turned(1, q)
        left_copy.start()

    def out_copies(q):
        target = tri_ref.at[
            pl.ds(x * h_count + q * hc, hc), :, pl.ds(pl.multiple_of(y * rows * chips, 128), rows * chips)
        ]
        copies = []
        for n, (device, owner) in enumerate(((across, y), (diagonal, 1 - y), (beside, 1 - y))):
            copies.append(
                pltpu.make_async_remote_copy(
                    src_ref=part.at[at_heads(q), at_rows(owner)],
                    dst_ref=target,
                    send_sem=out_send.at[n, q],
                    recv_sem=out_recv.at[n, q],
                    device_id=device,
                    device_id_type=MESH,
                )
            )
        own = pltpu.make_async_copy(part.at[at_heads(q), at_rows(y)], target, local_sem.at[q])
        return copies, own

    def collect(q):
        copies, own = out_copies(q)
        for copy in copies:
            copy.wait_recv()
        own.wait()
        for side in range(2):
            first = side * h_count + q * hc
            by_row[:, first : first + hc, :] = jnp.swapaxes(
                tri_ref[first : first + hc].astype(jnp.float32), 0, 1
            )

    def finish_row(i, carry):
        values = by_row[i]
        mean = jnp.mean(values, axis=0, keepdims=True)
        centered = values - mean
        variance = jnp.mean(centered * centered, axis=0, keepdims=True)
        block = (centered * lax.rsqrt(variance + 1e-05) * gain_columns[:, :1]).astype(jnp.bfloat16)
        projected = lax.dot_general(
            block, w_out_ref[...], (((0,), (0,)), ((), ())), preferred_element_type=jnp.float32
        )
        for other in range(2):
            for there in range(half):
                source = (other * half + there) * 2 * rows
                target = pl.ds((there * 2 + other) * 2 * rows, 2 * rows)
                update_ref[i, target, :] = (
                    gate_ref[i, target, :] * projected[source : source + 2 * rows]
                ).astype(jnp.bfloat16)
        return carry

    waited = set()

    def arrived(way, q, d):
        if (way, q, d) not in waited:
            waited.add((way, q, d))

            @pl.when(exists(way, d))
            def _():
                ring_copy(way, q, d).wait_recv()
                sibling_copy(way, q, d).start()

    def compute(q):
        for d in range(1, reach + 1):
            for way in range(2):
                arrived(way, q, d)
        each_piece(q, lambda copy: copy.wait_recv())
        heads = at_heads(q)
        product = lax.dot_general(
            lefts[heads], held[heads], (((2,), (2,)), ((0,), (0,))), preferred_element_type=jnp.float32
        )
        part[heads] = product.astype(jnp.bfloat16)
        copies, own = out_copies(q)
        for copy in copies:
            copy.start()
        own.start()

    lax.fori_loop(0, rows, right_row, 0, unroll=2)
    gain_columns[...] = jnp.swapaxes(jnp.broadcast_to(out_gain_ref[...], gain_columns.shape), 0, 1)
    quarter = rows // 4
    tasks = [functools.partial(turn_right, q) for q in range(2, chunks)]
    tasks += [functools.partial(lax.fori_loop, n * quarter, (n + 1) * quarter, left_row, 0) for n in range(4)]
    tasks += [send_left]
    tasks += [functools.partial(lax.fori_loop, n * quarter, (n + 1) * quarter, gate_row, 0) for n in range(4)]

    order = line_order(chunks, reach)
    steps = len(order)
    done = 0
    for n in range(steps):
        if n < 2:
            turn_right(n)
        if n == 0:
            pl.semaphore_wait(barrier, partners)
        q, d = order[n]
        for way in range(2):
            if d > 1:
                arrived(way, q, d - 1)

            @pl.when(has_next[way] & exists(way, d - 1) if d > 1 else has_next[way])
            def _():
                ring_copy(way, q, d).start()

        if d == 1:
            sibling_copy(0, q, 0).start()
        if n >= 1:
            for task in tasks[:2]:
                task()
            tasks = tasks[2:]
        last = order.index((done, reach))
        if n >= last + 2 and n < steps - 1 and not tasks:
            if done == 0:
                left_copy.wait_recv()
            compute(done)
            if done:
                collect(done - 1)
            done += 1
    for task in tasks:
        task()
    if done == 0:
        left_copy.wait_recv()
    while done < chunks:
        compute(done)
        if done:
            collect(done - 1)
        done += 1
    collect(chunks - 1)
    lax.fori_loop(0, rows, finish_row, 0, unroll=2)
    for q, d in order:
        for way in range(2):

            @pl.when(has_next[way] & exists(way, d - 1) if d > 1 else has_next[way])
            def _():
                ring_copy(way, q, d).wait_send()

    for q in range(chunks):
        each_piece(q, lambda copy: copy.wait_send())
    left_copy.wait_send()
    for q in range(chunks):
        for copy in out_copies(q)[0]:
            copy.wait_send()


def triangle(chips, chunks, pair_act, residue_valid, in_gain, w_left, w_left_gate, w_right, w_right_gate, out_gain, w_out, w_out_gate):
    rows, depth, channels = pair_act.shape
    h_count = w_left.shape[1]
    half = chips // 2
    dma = pltpu.SemaphoreType.DMA
    vmem = pl.BlockSpec(memory_space=pltpu.VMEM)
    smem = pl.BlockSpec(memory_space=pltpu.SMEM)
    return pl.pallas_call(
        functools.partial(triangle_kernel, chips, chunks),
        out_shape=jax.ShapeDtypeStruct((rows, depth, w_out.shape[1]), jnp.bfloat16),
        in_specs=[smem] + [pl.BlockSpec(memory_space=pltpu.HBM)] * 10,
        out_specs=vmem,
        scratch_shapes=[
            pltpu.VMEM((2 * h_count, rows, chips * 2 * rows), jnp.bfloat16),
            pltpu.VMEM((rows, 2 * h_count, chips * 2 * rows), jnp.float32),
            pltpu.VMEM((rows, depth, w_out_gate.shape[1]), jnp.float32),
            pltpu.VMEM((1, 2 * h_count), jnp.float32),
            pltpu.VMEM((2 * h_count, 2 * h_count), jnp.float32),
            pltpu.VMEM(w_out.shape, jnp.bfloat16),
            pltpu.VMEM((rows, depth, channels), jnp.bfloat16),
            pltpu.VMEM((1, depth), jnp.int32),
            pltpu.VMEM((1, channels), jnp.float32),
            pltpu.VMEM(w_out_gate.shape, jnp.bfloat16),
            dma((10,)),
            pltpu.VMEM((rows, depth, channels), jnp.bfloat16),
            pltpu.VMEM((2, 2 * h_count, channels), jnp.bfloat16),
            pltpu.VMEM((2, rows, h_count, depth), jnp.float32),
            pltpu.VMEM((h_count, chips * rows, depth), jnp.bfloat16),
            pltpu.VMEM((h_count, 2 * rows, depth), jnp.bfloat16),
            pltpu.VMEM((h_count, 2 * rows, chips * rows), jnp.bfloat16),
            dma((2,)),
            dma((2, chunks, half)),
            dma((2, chunks, half)),
            dma((2, chunks, half)),
            dma((2, chunks, half)),
            dma((3, chunks)),
            dma((3, chunks)),
            dma((chunks,)),
        ],
        compiler_params=pltpu.CompilerParams(
            collective_id=0, has_side_effects=True, vmem_limit_bytes=60 * 1024 * 1024
        ),
    )(
        residue_valid,
        pair_act,
        residue_valid[None, :],
        in_gain[None, :],
        w_left.T,
        w_left_gate.T,
        w_right.T,
        w_right_gate.T,
        w_out_gate,
        out_gain[None, :],
        w_out,
    )


def finish(tri_full, out_gain, w_out):
    tri_norm = norm_axis(tri_full.astype(jnp.float32), out_gain[:, None, None], 0).astype(jnp.bfloat16)
    return jnp.einsum("hij,hc->ijc", tri_norm, w_out, preferred_element_type=jnp.float32)


def ring_body(chips, *operands):
    return triangle(chips, CHUNKS, *operands)


def body(*operands):
    pair_act, residue_valid, in_gain, w_left, w_left_gate, w_right, w_right_gate, out_gain, w_out, w_out_gate = operands
    row_count = pair_act.shape[0]
    col_count = pair_act.shape[1]
    row_first = lax.axis_index("row") * row_count
    col_first = lax.axis_index("sub") * col_count
    normed = norm_axis(pair_act.astype(jnp.float32), in_gain, 2).astype(jnp.bfloat16)
    valid = residue_valid.astype(jnp.float32)
    row_valid = lax.dynamic_slice_in_dim(valid, row_first, row_count)
    col_valid = lax.dynamic_slice_in_dim(valid, col_first, col_count)
    weight = (row_valid[:, None] * col_valid[None, :])[None, :, :]

    def project(w_lin, w_gate):
        linear = jnp.einsum("ikc,ch->hik", normed, w_lin, preferred_element_type=jnp.float32)
        gating = jnp.einsum("ikc,ch->hik", normed, w_gate, preferred_element_type=jnp.float32)
        return (jax.nn.sigmoid(gating) * linear * weight).astype(jnp.bfloat16)

    left = project(w_left, w_left_gate)
    right = project(w_right, w_right_gate)
    right_all = lax.all_gather(right, "row", axis=1, tiled=True)
    partial_tri = lax.dot_general(
        left, right_all, (((2,), (2,)), ((0,), (0,))), preferred_element_type=jnp.float32
    )
    tri_half = lax.psum_scatter(partial_tri.astype(jnp.bfloat16), "sub", scatter_dimension=2, tiled=True)
    tri_full = lax.all_gather(tri_half, "chan", axis=0, tiled=True)
    gating = jnp.einsum("ijc,cd->ijd", normed, w_out_gate, preferred_element_type=jnp.float32)
    return (jax.nn.sigmoid(gating) * finish(tri_full, out_gain, w_out)).astype(jnp.bfloat16)


def solution(mesh):
    placed = (
        P(("groups", "row"), "sub", None),
        P("groups"),
        P(),
        P(None, "chan"),
        P(None, "chan"),
        P(None, "chan"),
        P(None, "chan"),
        P(),
        P(),
        P(),
    )
    rows, chan, sub = (mesh.shape[name] for name in ("row", "chan", "sub"))
    ringed = sub == 1 and chan == 2 and rows % 8 == 0
    return jax.shard_map(
        functools.partial(ring_body, rows // 2) if ringed else body,
        mesh=mesh,
        in_specs=placed,
        out_specs=P(("groups", "row"), "sub", None),
        check_vma=False,
    )
```

```python
import functools

import jax
import jax.numpy as jnp
from jax import lax
from jax.experimental import pallas as pl
from jax.experimental.pallas import tpu as pltpu
from jax.sharding import PartitionSpec as P

CHUNKS = 8
GROUP = 4
MESH = pl.DeviceIdType.MESH


def norm_axis(values, gain, axis):
    mean = jnp.mean(values, axis=axis, keepdims=True)
    centered = values - mean
    variance = jnp.mean(centered * centered, axis=axis, keepdims=True)
    return centered * lax.rsqrt(variance + 1e-05) * gain


def line_order(chunks, reach):
    order = []
    for first in range(0, chunks, GROUP):
        pair = range(first, min(first + GROUP, chunks))
        block = [(q, d) for d in range(1, reach + 1) for q in pair]
        if order:
            tail = order.pop()
            order += [block[0], tail] + block[1:]
        else:
            order = block
    return order


def triangle_kernel(
    chips,
    chunks,
    row_valid_ref,
    pair_hbm,
    col_valid_hbm,
    in_gain_hbm,
    w_left_hbm,
    w_left_gate_hbm,
    w_right_hbm,
    w_right_gate_hbm,
    w_out_gate_hbm,
    out_gain_hbm,
    w_out_hbm,
    update_ref,
    tri_ref,
    by_row,
    gate_ref,
    out_gain_ref,
    gain_columns,
    w_out_ref,
    pair_ref,
    col_valid_ref,
    in_gain_ref,
    w_out_gate_ref,
    load_sem,
    normed,
    weights,
    staged,
    held,
    lefts,
    part,
    sib_sem,
    ring_send,
    ring_recv,
    pair_send,
    pair_recv,
    out_send,
    out_recv,
    local_sem,
):
    rows = pair_hbm.shape[0]
    h_count = w_left_hbm.shape[0]
    hc = h_count // chunks
    half = chips // 2
    loads = [
        pltpu.make_async_copy(source, target, load_sem.at[n])
        for n, (source, target) in enumerate(
            (
                (pair_hbm, pair_ref),
                (in_gain_hbm, in_gain_ref),
                (col_valid_hbm, col_valid_ref),
                (w_right_hbm, weights.at[0, :h_count]),
                (w_right_gate_hbm, weights.at[0, h_count:]),
                (w_left_hbm, weights.at[1, :h_count]),
                (w_left_gate_hbm, weights.at[1, h_count:]),
                (w_out_gate_hbm, w_out_gate_ref),
                (out_gain_hbm, out_gain_ref),
                (w_out_hbm, w_out_ref),
            )
        )
    ]
    for load in loads:
        load.start()
    index = lax.axis_index("row")
    x = lax.axis_index("chan")
    core = lax.rem(index, 2)
    chip = lax.div(index, 2)
    y = lax.rem(chip, 2)
    z = lax.div(chip, 2)
    reach = half - 1
    sibling = {"row": chip * 2 + (1 - core), "chan": x}
    nexts = [{"row": index + 4, "chan": x}, {"row": index - 4, "chan": x}]
    has_next = [z < half - 1, z > 0]
    beside = {"row": (2 * z + 1 - y) * 2 + core, "chan": x}
    across = {"row": index, "chan": 1 - x}
    diagonal = {"row": (2 * z + 1 - y) * 2 + core, "chan": 1 - x}

    barrier = pltpu.get_barrier_semaphore()
    for partner in (sibling, beside, across, diagonal):
        pl.semaphore_signal(barrier, inc=1, device_id=partner, device_id_type=MESH)
    for way in range(2):

        @pl.when(has_next[way])
        def _():
            pl.semaphore_signal(barrier, inc=1, device_id=nexts[way], device_id_type=MESH)

    partners = 4 + jnp.where(z < half - 1, 1, 0) + jnp.where(z > 0, 1, 0)

    def at_rows(block):
        return pl.ds(pl.multiple_of(block * rows, rows), rows)

    def at_heads(q):
        return pl.ds(q * hc, hc)

    for load in loads:
        load.wait()
    col_valid = col_valid_ref[...].astype(jnp.float32)

    def project(i, side, block):
        both = lax.dot_general(
            weights[side], block, (((1,), (1,)), ((), ())), preferred_element_type=jnp.float32
        )
        weight = col_valid * row_valid_ref[index * rows + i].astype(jnp.float32)
        staged[side, i] = jax.nn.sigmoid(both[h_count:]) * both[:h_count] * weight

    def right_row(i, carry):
        values = pair_ref[i].astype(jnp.float32)
        mean = jnp.mean(values, axis=1, keepdims=True)
        centered = values - mean
        variance = jnp.mean(centered * centered, axis=1, keepdims=True)
        block = (centered * lax.rsqrt(variance + 1e-05) * in_gain_ref[...]).astype(jnp.bfloat16)
        normed[i] = block
        project(i, 0, block)
        return carry

    def left_row(i, carry):
        project(i, 1, normed[i])
        return carry

    def gate_row(i, carry):
        gate_ref[i] = jax.nn.sigmoid(
            jnp.dot(normed[i], w_out_gate_ref[...], preferred_element_type=jnp.float32)
        )
        return carry

    def turned(side, q):
        return jnp.swapaxes(staged[side, :, q * hc : (q + 1) * hc, :], 0, 1).astype(jnp.bfloat16)

    def turn_right(q):
        held[at_heads(q), at_rows(2 * z + core)] = turned(0, q)


    def origin(way, d):
        return z - (1 - 2 * way) * d

    def exists(way, d):
        return origin(way, d) >= 0 if way == 0 else origin(way, d) < half

    def ring_copy(way, q, d):
        spot = held.at[at_heads(q), at_rows(2 * origin(way, d - 1) + core)]
        return pltpu.make_async_remote_copy(
            src_ref=spot,
            dst_ref=spot,
            send_sem=ring_send.at[way, q, d - 1],
            recv_sem=ring_recv.at[way, q, d - 1],
            device_id=nexts[way],
            device_id_type=MESH,
        )

    def sibling_copy(way, q, d):
        spot = held.at[at_heads(q), at_rows(2 * origin(way, d) + core)]
        return pltpu.make_async_remote_copy(
            src_ref=spot,
            dst_ref=spot,
            send_sem=pair_send.at[way, q, d],
            recv_sem=pair_recv.at[way, q, d],
            device_id=sibling,
            device_id_type=MESH,
        )

    def each_piece(q, act):
        act(sibling_copy(0, q, 0))
        for way in range(2):
            for d in range(1, reach + 1):

                @pl.when(exists(way, d))
                def _():
                    act(sibling_copy(way, q, d))

    left_spot = lefts.at[:, at_rows(y)]
    left_copy = pltpu.make_async_remote_copy(
        src_ref=left_spot,
        dst_ref=left_spot,
        send_sem=sib_sem.at[0],
        recv_sem=sib_sem.at[1],
        device_id=beside,
        device_id_type=MESH,
    )

    def send_left():
        for q in range(chunks):
            lefts[at_heads(q), at_rows(y)] = turned(1, q)
        left_copy.start()

    def out_copies(q):
        target = tri_ref.at[
            pl.ds(x * h_count + q * hc, hc), :, pl.ds(pl.multiple_of(y * rows * chips, 128), rows * chips)
        ]
        copies = []
        for n, (device, owner) in enumerate(((across, y), (diagonal, 1 - y), (beside, 1 - y))):
            copies.append(
                pltpu.make_async_remote_copy(
                    src_ref=part.at[at_heads(q), at_rows(owner)],
                    dst_ref=target,
                    send_sem=out_send.at[n, q],
                    recv_sem=out_recv.at[n, q],
                    device_id=device,
                    device_id_type=MESH,
                )
            )
        own = pltpu.make_async_copy(part.at[at_heads(q), at_rows(y)], target, local_sem.at[q])
        return copies, own

    def collect(q):
        copies, own = out_copies(q)
        for copy in copies:
            copy.wait_recv()
        own.wait()
        for side in range(2):
            first = side * h_count + q * hc
            by_row[:, first : first + hc, :] = jnp.swapaxes(
                tri_ref[first : first + hc].astype(jnp.float32), 0, 1
            )

    def finish_row(i, carry):
        values = by_row[i]
        mean = jnp.mean(values, axis=0, keepdims=True)
        centered = values - mean
        variance = jnp.mean(centered * centered, axis=0, keepdims=True)
        block = (centered * lax.rsqrt(variance + 1e-05) * gain_columns[:, :1]).astype(jnp.bfloat16)
        projected = lax.dot_general(
            block, w_out_ref[...], (((0,), (0,)), ((), ())), preferred_element_type=jnp.float32
        )
        for other in range(2):
            for there in range(half):
                source = (other * half + there) * 2 * rows
                target = pl.ds((there * 2 + other) * 2 * rows, 2 * rows)
                update_ref[i, target, :] = (
                    gate_ref[i, target, :] * projected[source : source + 2 * rows]
                ).astype(jnp.bfloat16)
        return carry

    waited = set()

    def arrived(way, q, d):
        if (way, q, d) not in waited:
            waited.add((way, q, d))

            @pl.when(exists(way, d))
            def _():
                ring_copy(way, q, d).wait_recv()
                sibling_copy(way, q, d).start()

    def compute(q):
        for d in range(1, reach + 1):
            for way in range(2):
                arrived(way, q, d)
        each_piece(q, lambda copy: copy.wait_recv())
        heads = at_heads(q)
        product = lax.dot_general(
            lefts[heads], held[heads], (((2,), (2,)), ((0,), (0,))), preferred_element_type=jnp.float32
        )
        part[heads] = product.astype(jnp.bfloat16)
        copies, own = out_copies(q)
        for copy in copies:
            copy.start()
        own.start()

    lax.fori_loop(0, rows, right_row, 0, unroll=2)
    gain_columns[...] = jnp.swapaxes(jnp.broadcast_to(out_gain_ref[...], gain_columns.shape), 0, 1)
    quarter = rows // 4
    tasks = [functools.partial(turn_right, q) for q in range(GROUP, chunks)]
    tasks += [functools.partial(lax.fori_loop, n * quarter, (n + 1) * quarter, left_row, 0) for n in range(4)]
    tasks += [send_left]
    tasks += [functools.partial(lax.fori_loop, n * quarter, (n + 1) * quarter, gate_row, 0) for n in range(4)]

    order = line_order(chunks, reach)
    steps = len(order)
    done = 0
    for n in range(steps):
        if n < GROUP:
            turn_right(n)
        if n == 0:
            pl.semaphore_wait(barrier, partners)
        q, d = order[n]
        for way in range(2):
            if d > 1:
                arrived(way, q, d - 1)

            @pl.when(has_next[way] & exists(way, d - 1) if d > 1 else has_next[way])
            def _():
                ring_copy(way, q, d).start()

        if d == 1:
            sibling_copy(0, q, 0).start()
        if n >= 1:
            for task in tasks[:1]:
                task()
            tasks = tasks[1:]
        last = order.index((done, reach))
        if n >= last + 2 and n < steps - 1 and not tasks:
            if done == 0:
                left_copy.wait_recv()
            compute(done)
            if done:
                collect(done - 1)
            done += 1
    for task in tasks:
        task()
    if done == 0:
        left_copy.wait_recv()
    while done < chunks:
        compute(done)
        if done:
            collect(done - 1)
        done += 1
    collect(chunks - 1)
    lax.fori_loop(0, rows, finish_row, 0, unroll=2)
    for q, d in order:
        for way in range(2):

            @pl.when(has_next[way] & exists(way, d - 1) if d > 1 else has_next[way])
            def _():
                ring_copy(way, q, d).wait_send()

    for q in range(chunks):
        each_piece(q, lambda copy: copy.wait_send())
    left_copy.wait_send()
    for q in range(chunks):
        for copy in out_copies(q)[0]:
            copy.wait_send()


def triangle(chips, chunks, pair_act, residue_valid, in_gain, w_left, w_left_gate, w_right, w_right_gate, out_gain, w_out, w_out_gate):
    rows, depth, channels = pair_act.shape
    h_count = w_left.shape[1]
    half = chips // 2
    dma = pltpu.SemaphoreType.DMA
    vmem = pl.BlockSpec(memory_space=pltpu.VMEM)
    smem = pl.BlockSpec(memory_space=pltpu.SMEM)
    return pl.pallas_call(
        functools.partial(triangle_kernel, chips, chunks),
        out_shape=jax.ShapeDtypeStruct((rows, depth, w_out.shape[1]), jnp.bfloat16),
        in_specs=[smem] + [pl.BlockSpec(memory_space=pltpu.HBM)] * 10,
        out_specs=vmem,
        scratch_shapes=[
            pltpu.VMEM((2 * h_count, rows, chips * 2 * rows), jnp.bfloat16),
            pltpu.VMEM((rows, 2 * h_count, chips * 2 * rows), jnp.float32),
            pltpu.VMEM((rows, depth, w_out_gate.shape[1]), jnp.float32),
            pltpu.VMEM((1, 2 * h_count), jnp.float32),
            pltpu.VMEM((2 * h_count, 2 * h_count), jnp.float32),
            pltpu.VMEM(w_out.shape, jnp.bfloat16),
            pltpu.VMEM((rows, depth, channels), jnp.bfloat16),
            pltpu.VMEM((1, depth), jnp.int32),
            pltpu.VMEM((1, channels), jnp.float32),
            pltpu.VMEM(w_out_gate.shape, jnp.bfloat16),
            dma((10,)),
            pltpu.VMEM((rows, depth, channels), jnp.bfloat16),
            pltpu.VMEM((2, 2 * h_count, channels), jnp.bfloat16),
            pltpu.VMEM((2, rows, h_count, depth), jnp.float32),
            pltpu.VMEM((h_count, chips * rows, depth), jnp.bfloat16),
            pltpu.VMEM((h_count, 2 * rows, depth), jnp.bfloat16),
            pltpu.VMEM((h_count, 2 * rows, chips * rows), jnp.bfloat16),
            dma((2,)),
            dma((2, chunks, half)),
            dma((2, chunks, half)),
            dma((2, chunks, half)),
            dma((2, chunks, half)),
            dma((3, chunks)),
            dma((3, chunks)),
            dma((chunks,)),
        ],
        compiler_params=pltpu.CompilerParams(
            collective_id=0, has_side_effects=True, vmem_limit_bytes=60 * 1024 * 1024
        ),
    )(
        residue_valid,
        pair_act,
        residue_valid[None, :],
        in_gain[None, :],
        w_left.T,
        w_left_gate.T,
        w_right.T,
        w_right_gate.T,
        w_out_gate,
        out_gain[None, :],
        w_out,
    )


def finish(tri_full, out_gain, w_out):
    tri_norm = norm_axis(tri_full.astype(jnp.float32), out_gain[:, None, None], 0).astype(jnp.bfloat16)
    return jnp.einsum("hij,hc->ijc", tri_norm, w_out, preferred_element_type=jnp.float32)


def ring_body(chips, *operands):
    return triangle(chips, CHUNKS, *operands)


def body(*operands):
    pair_act, residue_valid, in_gain, w_left, w_left_gate, w_right, w_right_gate, out_gain, w_out, w_out_gate = operands
    row_count = pair_act.shape[0]
    col_count = pair_act.shape[1]
    row_first = lax.axis_index("row") * row_count
    col_first = lax.axis_index("sub") * col_count
    normed = norm_axis(pair_act.astype(jnp.float32), in_gain, 2).astype(jnp.bfloat16)
    valid = residue_valid.astype(jnp.float32)
    row_valid = lax.dynamic_slice_in_dim(valid, row_first, row_count)
    col_valid = lax.dynamic_slice_in_dim(valid, col_first, col_count)
    weight = (row_valid[:, None] * col_valid[None, :])[None, :, :]

    def project(w_lin, w_gate):
        linear = jnp.einsum("ikc,ch->hik", normed, w_lin, preferred_element_type=jnp.float32)
        gating = jnp.einsum("ikc,ch->hik", normed, w_gate, preferred_element_type=jnp.float32)
        return (jax.nn.sigmoid(gating) * linear * weight).astype(jnp.bfloat16)

    left = project(w_left, w_left_gate)
    right = project(w_right, w_right_gate)
    right_all = lax.all_gather(right, "row", axis=1, tiled=True)
    partial_tri = lax.dot_general(
        left, right_all, (((2,), (2,)), ((0,), (0,))), preferred_element_type=jnp.float32
    )
    tri_half = lax.psum_scatter(partial_tri.astype(jnp.bfloat16), "sub", scatter_dimension=2, tiled=True)
    tri_full = lax.all_gather(tri_half, "chan", axis=0, tiled=True)
    gating = jnp.einsum("ijc,cd->ijd", normed, w_out_gate, preferred_element_type=jnp.float32)
    return (jax.nn.sigmoid(gating) * finish(tri_full, out_gain, w_out)).astype(jnp.bfloat16)


def solution(mesh):
    placed = (
        P(("groups", "row"), "sub", None),
        P("groups"),
        P(),
        P(None, "chan"),
        P(None, "chan"),
        P(None, "chan"),
        P(None, "chan"),
        P(),
        P(),
        P(),
    )
    rows, chan, sub = (mesh.shape[name] for name in ("row", "chan", "sub"))
    ringed = sub == 1 and chan == 2 and rows % 8 == 0
    return jax.shard_map(
        functools.partial(ring_body, rows // 2) if ringed else body,
        mesh=mesh,
        in_specs=placed,
        out_specs=P(("groups", "row"), "sub", None),
        check_vma=False,
    )
```
